256 devices in a mesh: animal: 8 (over x, core), marker: 32 (over y, z).
Axes of the slice: x: 4, y: 4, z: 8, core: 2. Of those that a mesh axis runs over, the one named last changes fastest.
Arguments:
- genotype: float32 [12288, 49152], P('animal', 'marker'), may hold values from 0 to 2, as said below
- allele_freq: float32 [49152], P('marker'), may hold values from 0.05 to 0.5
- shrink: float32 [49152], P('marker'), may hold values from 0.05 to 0.6
- right_side: float32 [32, 49152], P(None, 'marker'), may hold values from -6 to 6
Outputs:
- solution: float32 [32, 49152], P(None, 'marker')
- residual: float32 [32, 49152], P(None, 'marker')
The draws below stay inside these ranges and needn't reach their ends.
Inputs may be any that keep to these rules, and one draw needn't show every extreme that they name: genotype codes are 0, 1 or 2.
All inputs are finite; a program needn't handle non-finite values.
Results may differ from the reference program's by a relative error of at most 0.002.
Values sent between devices are 32-bit elements; how exact they have to be, the bound alone decides.
No kernel may reach another device: no remote copies, remote signals or barrier semaphores. Data moves between devices by JAX's collectives and lax.ppermute only.
A program may use at most 64 MiB of HBM per device.

```python
import math
import jax
import jax.numpy as jnp
from jax import lax

M = 49152
RHS = 32
ITERS = 4
ANIMALS = 12288


def shared_freq(key):
    return jax.random.uniform(jax.random.fold_in(key, 11), (M,), jnp.float32, 0.05, 0.5)


def draw_allele_freq(key, part):
    return shared_freq(key)


def draw_genotype(key, part):
    freq_row = shared_freq(key)[None, :]
    uniform_vals = jax.random.uniform(jax.random.fold_in(key, 23), (ANIMALS, M), jnp.float32)
    low_cut = (1.0 - freq_row) * (1.0 - freq_row)
    high_cut = 1.0 - freq_row * freq_row
    codes = (uniform_vals > low_cut).astype(jnp.float32) + (uniform_vals > high_cut).astype(jnp.float32)
    return codes


def level_of(rng, extent, split, smallest, top_value):
    level, own = 1.0, jax.random.fold_in(rng, 6)
    for position, shards_of in split:
        heights = jnp.exp(jax.random.uniform(jax.random.fold_in(own, position), (shards_of,), jnp.float32, smallest / len(split), top_value / len(split)))
        level = level * jnp.repeat(heights, extent[position] // shards_of).reshape([-1 if axis == position else 1 for axis in range(len(extent))])
    return level


def gaussian(rng, extent, spread, most, shards=(), dtype=jnp.bfloat16):
    drawn = spread * jax.random.normal(rng, extent, jnp.float32)
    if shards:
        drawn = drawn * level_of(rng, extent, shards, -0.22, 0.18)
    return jnp.clip(drawn, -most, most).astype(dtype)


def setup_inputs(seed: int = 0) -> dict:
    streams_of = jax.random.split(jax.random.key(seed), 5)
    genotype = draw_genotype(jax.random.fold_in(streams_of[4], 71), 0)
    allele_freq = draw_allele_freq(jax.random.fold_in(streams_of[4], 71), 0)
    shrink = jnp.clip(jnp.exp(math.log(0.6) - 2.4849067 * jax.random.uniform(streams_of[2], (M,), jnp.float32) ** level_of(streams_of[2], (M,), ((0, 32),), -0.2, 0.2)), 0.05, 0.6)
    right_side = gaussian(streams_of[3], (RHS, M), 1.0, 6.0, ((1, 32),), jnp.float32)
    return {"genotype": genotype, "allele_freq": allele_freq, "shrink": shrink, "right_side": right_side}


def operator(direction, genotype, allele_freq, shrink):
    offset = jnp.sum(2.0 * allele_freq[None, :] * direction, axis=1)
    row_part = lax.dot_general(direction, genotype, (((1,), (1,)), ((), ())), precision=lax.Precision.HIGHEST, preferred_element_type=jnp.float32)
    row_values = row_part - offset[:, None]
    col_terms = jnp.dot(row_values, genotype, precision=lax.Precision.HIGHEST, preferred_element_type=jnp.float32)
    row_total = jnp.sum(row_values, axis=1)
    inv_count = jnp.float32(1.0) / jnp.float32(ANIMALS)
    return (col_terms - 2.0 * allele_freq[None, :] * row_total[:, None]) * inv_count + shrink[None, :] * direction


def reference(genotype, allele_freq, shrink, right_side):
    precond = 2.0 * allele_freq * (1.0 - allele_freq) + shrink
    solution = jnp.zeros_like(right_side)
    residual = right_side
    scaled = residual / precond[None, :]
    direction = scaled
    rho_now = jnp.sum(residual * scaled, axis=1)
    for step in range(ITERS):
        image = operator(direction, genotype, allele_freq, shrink)
        curve = jnp.sum(direction * image, axis=1)
        step_len = rho_now / curve
        solution = solution + step_len[:, None] * direction
        residual = residual - step_len[:, None] * image
        scaled = residual / precond[None, :]
        rho_new = jnp.sum(residual * scaled, axis=1)
        direction = scaled + (rho_new / rho_now)[:, None] * direction
        rho_now = rho_new
    return solution, residual
```

```python
import jax
import jax.numpy as jnp
from jax import lax
from jax.sharding import PartitionSpec as P

ITERS = 4


def split2(v):
    hi = lax.reduce_precision(v, 8, 7)
    lo = lax.reduce_precision(v - hi, 8, 7)
    return jnp.concatenate([hi, lo], axis=0).astype(jnp.bfloat16)


def body(genotype, allele_freq, shrink, right_side):
    cores = 2
    xs = lax.axis_size("animal") // cores
    count = genotype.shape[0] * lax.axis_size("animal")
    inv_count = jnp.float32(1.0) / jnp.float32(count)
    rhs, width = right_side.shape
    geno = genotype.astype(jnp.bfloat16)
    twice = 2.0 * allele_freq[None, :]
    own_shrink = shrink[None, :]
    precond = 2.0 * allele_freq * (1.0 - allele_freq) + shrink
    precond = precond[None, :]

    def product(vec, dim):
        both = lax.dot_general(
            split2(vec), geno, (((1,), (dim,)), ((), ())), preferred_element_type=jnp.float32
        )
        return both[:rhs] + both[rhs:]

    def extend(main, scalars):
        pad = jnp.stack(scalars, axis=1)
        pad = jnp.pad(pad, ((0, 0), (0, 128 - len(scalars))))
        return jnp.concatenate([main, pad], axis=1)

    def marker_sum(part):
        got = lax.all_to_all(part, "marker", 0, 0, tiled=True)
        total = jnp.sum(got, axis=0, keepdims=True)
        return lax.all_to_all(jnp.broadcast_to(total, part.shape), "marker", 0, 0, tiled=True)

    def animal_sum(part):
        swap = [(x * cores + c, x * cores + 1 - c) for x in range(xs) for c in range(cores)]
        part = part + lax.ppermute(part, "animal", swap)
        moved = [
            lax.ppermute(
                part,
                "animal",
                [(x * cores + c, (x + d) % xs * cores + c) for x in range(xs) for c in range(cores)],
            )
            for d in range(1, xs)
        ]
        return part + sum(moved[1:], moved[0])

    residual = right_side
    solution = jnp.zeros_like(residual)
    direction = jnp.zeros_like(residual)
    row_values = jnp.zeros((rhs, genotype.shape[0]), jnp.float32)
    rho = None
    for step in range(ITERS):
        scaled = residual / precond
        part = product(scaled, 1) - jnp.sum(twice * scaled, axis=1)[:, None]
        weighted = own_shrink * scaled
        scalars = [
            jnp.sum(residual * scaled, axis=1),
            jnp.sum(weighted * scaled, axis=1),
            jnp.sum(weighted * direction, axis=1),
        ]
        total = marker_sum(extend(part, scalars))
        new_rows = total[:, : part.shape[1]]
        new_rho, square, cross = (total[:, part.shape[1] + i] for i in range(3))
        if step == 0:
            direction, row_values, shrunk = scaled, new_rows, square
        else:
            beta = new_rho / rho
            direction = scaled + beta[:, None] * direction
            row_values = new_rows + beta[:, None] * row_values
            shrunk = square + beta * (2.0 * cross + beta * shrunk)
        rho = new_rho
        cols = product(row_values, 0) - twice * jnp.sum(row_values, axis=1)[:, None]
        total = animal_sum(extend(cols, [jnp.sum(row_values * row_values, axis=1)]))
        image = total[:, :width] * inv_count + own_shrink * direction
        curve = total[:, width] * inv_count + shrunk
        step_len = (rho / curve)[:, None]
        solution = solution + step_len * direction
        residual = residual - step_len * image
    return solution, residual


def solution(mesh):
    placed = (P("animal", "marker"), P("marker"), P("marker"), P(None, "marker"))
    return jax.shard_map(
        body,
        mesh=mesh,
        in_specs=placed,
        out_specs=(P(None, "marker"), P(None, "marker")),
        check_vma=False,
    )
```

```python
import functools

import jax
import jax.numpy as jnp
from jax import lax
from jax.experimental import pallas as pl
from jax.experimental.pallas import tpu as pltpu
from jax.sharding import PartitionSpec as P

ITERS = 4
CORES = 2
EXTRA = 128
BLOCK = 256
AHEAD = 2
MIB = 1024 * 1024
VMEM = pl.BlockSpec(memory_space=pltpu.VMEM)
ANY = pl.BlockSpec(memory_space=pl.ANY)


def half_slices(half):
    core = lax.axis_index("animal") % CORES
    return pl.ds(core * half, half), pl.ds((1 - core) * half, half)


def lanes(*columns):
    at = lax.broadcasted_iota(jnp.int32, (columns[0].shape[0], EXTRA), 1)
    out = jnp.zeros(at.shape, jnp.float32)
    for i, column in enumerate(columns):
        out = jnp.where(at == i, column, out)
    return out


def put_terms(v, terms_ref):
    rows = v.shape[0]
    hi = v.astype(jnp.bfloat16)
    terms_ref[:rows] = hi
    terms_ref[rows:] = (v - hi.astype(jnp.float32)).astype(jnp.bfloat16)


def row_sum(v):
    return jnp.sum(v, axis=1, keepdims=True)


def folded(both):
    half = both.shape[0] // 2
    return both[:half] + both[half:]


def row_product(terms_ref, block):
    return folded(
        lax.dot_general(terms_ref[...], block, (((1,), (1,)), ((), ())), preferred_element_type=jnp.float32)
    )


def col_product(terms_ref, block):
    return folded(jnp.dot(terms_ref[...], block, preferred_element_type=jnp.float32))


def blocks(extent):
    return [pl.ds(i * BLOCK, BLOCK) for i in range(extent // BLOCK)]


def first_kernel(
    geno_ref, freq_ref, shrink_ref, right_ref,
    coded_ref, freq_out, shrink_out, residual_out, scaled_out, part_ref,
    stage, right, freq_line, shrink_line, terms_ref, geno_sems, small_sems,
):
    animals = coded_ref.shape[0]
    half = right_ref.shape[0] // 2
    pairs = ((right_ref, right), (freq_ref, freq_line), (shrink_ref, shrink_line))
    small = [pltpu.make_async_copy(src, dst, small_sems.at[i]) for i, (src, dst) in enumerate(pairs)]
    spots = blocks(animals)
    copies = [
        pltpu.make_async_copy(geno_ref.at[at, :], stage.at[at, :], geno_sems.at[i]) for i, at in enumerate(spots)
    ]
    for copy in small + copies[:AHEAD]:
        copy.start()
    for copy in small:
        copy.wait()
    freq = freq_line[...].reshape(1, -1)
    shrink = shrink_line[...].reshape(1, -1)
    freq_out[...] = freq
    shrink_out[...] = shrink
    mine, other = half_slices(half)
    precond = 2.0 * freq * (1.0 - freq) + shrink
    residual_out[:half] = right[mine, :]
    residual_out[half:] = right[other, :]
    scaled_out[...] = residual_out[...] / precond
    residual = right[...]
    scaled = residual / precond
    extra = lanes(row_sum(residual * scaled), row_sum(shrink * scaled * scaled))
    part_ref[:, :, animals:] = extra[:, None, :]
    put_terms(scaled, terms_ref)
    offset = row_sum(2.0 * freq * scaled)
    for i, at in enumerate(spots):
        copies[i].wait()
        if i + AHEAD < len(copies):
            copies[i + AHEAD].start()
        block = stage[at, :].astype(jnp.bfloat16)
        coded_ref[at, :] = block
        part_ref[:, :, at] = (row_product(terms_ref, block) - offset)[:, None, :]


def spread_kernel(got_ref, out_ref):
    out_ref[...] = jnp.broadcast_to(jnp.sum(got_ref[...], axis=0, keepdims=True), out_ref.shape)


def add_kernel(*refs):
    *ins, out_ref = refs
    total = ins[0][...]
    for ref in ins[1:]:
        total += ref[...]
    out_ref[...] = total


def half_columns(vec, coded_ref, freq_ref, out_ref, terms_ref):
    width = coded_ref.shape[1]
    put_terms(vec, terms_ref)
    row_total = row_sum(vec)
    for at in blocks(width):
        out_ref[:, at] = col_product(terms_ref, coded_ref[:, at]) - 2.0 * freq_ref[:, at] * row_total
    out_ref[:, width:] = lanes(row_sum(vec * vec))


def other_columns(first, total_ref, freq_ref, coded_ref, *refs):
    *old, out_ref, terms_ref = refs
    animals = coded_ref.shape[0]
    half = out_ref.shape[0]
    total = total_ref[half_slices(half)[1], 0, :]
    vec = total[:, :animals]
    if not first:
        rows_ref, kept_ref = old
        beta = total[:, animals : animals + 1] / kept_ref[half:, :1]
        vec += beta * rows_ref[half:, :]
    half_columns(vec, coded_ref, freq_ref, out_ref, terms_ref)


def mine_columns(first, total_ref, freq_ref, coded_ref, scaled_ref, *refs):
    *old, direction_out, rows_out, kept_out, out_ref, terms_ref = refs
    animals = coded_ref.shape[0]
    half = out_ref.shape[0]
    for local, at in zip((slice(0, half), slice(half, None)), half_slices(half)):
        total = total_ref[at, 0, :]
        vec = total[:, :animals]
        rho, square, cross = (total[:, animals + i : animals + i + 1] for i in range(3))
        if first:
            direction_out[local] = scaled_ref[local]
            kept_out[local] = lanes(rho, square)
        else:
            direction_ref, rows_ref, kept_ref = old
            beta = rho / kept_ref[local, :1]
            vec += beta * rows_ref[local]
            direction_out[local] = scaled_ref[local] + beta * direction_ref[local]
            kept_out[local] = lanes(rho, square + beta * (2.0 * cross + beta * kept_ref[local, 1:2]))
        rows_out[local] = vec
    half_columns(rows_out[:half], coded_ref, freq_ref, out_ref, terms_ref)


def update(inv_count, local, total_ref, shrink_ref, direction_ref, residual_ref, kept_ref, solution_ref=None):
    width = direction_ref.shape[1]
    direction = direction_ref[local]
    image = total_ref[:, :width] * inv_count + shrink_ref[...] * direction
    curve = total_ref[:, width : width + 1] * inv_count + kept_ref[local, 1:2]
    step = kept_ref[local, :1] / curve
    moved = step * direction
    if solution_ref is not None:
        moved += solution_ref[local]
    return moved, residual_ref[local] - step * image, direction


def half_rows(inv_count, local, state, freq_ref, coded_ref, solution_out, residual_out, scaled_out, write, terms_ref):
    animals = coded_ref.shape[0]
    solution, residual, direction = update(inv_count, local, *state)
    freq, shrink = freq_ref[...], state[1][...]
    scaled = residual / (2.0 * freq * (1.0 - freq) + shrink)
    solution_out[...] = solution
    residual_out[...] = residual
    scaled_out[...] = scaled
    put_terms(scaled, terms_ref)
    weighted = shrink * scaled
    offset = row_sum(2.0 * freq * scaled)
    for at in blocks(animals):
        write(at, row_product(terms_ref, coded_ref[at, :]) - offset)
    write(
        pl.ds(animals, EXTRA),
        lanes(row_sum(residual * scaled), row_sum(weighted * scaled), row_sum(weighted * direction)),
    )


def mine_rows(inv_count, freq_ref, coded_ref, *refs):
    *state, solution_out, residual_out, scaled_out, part_ref, terms_ref = refs
    half = part_ref.shape[0]

    def write(at, value):
        part_ref[:, :, at] = value[:, None, :]

    half_rows(
        inv_count, slice(0, half), state, freq_ref, coded_ref,
        solution_out, residual_out, scaled_out, write, terms_ref,
    )


def other_rows(inv_count, freq_ref, coded_ref, solution_ref, residual_ref, scaled_ref, half_ref, *refs):
    *state, solution_out, residual_out, scaled_out, part_ref, terms_ref = refs
    half = half_ref.shape[0]
    mine, other = half_slices(half)
    part_ref[mine] = half_ref[...]
    solution_out[:half] = solution_ref[...]
    residual_out[:half] = residual_ref[...]
    scaled_out[:half] = scaled_ref[...]

    def write(at, value):
        part_ref[other, :, at] = value[:, None, :]

    top = slice(half, None)
    half_rows(
        inv_count, top, state, freq_ref, coded_ref,
        solution_out.at[top], residual_out.at[top], scaled_out.at[top], write, terms_ref,
    )


def last_kernel(inv_count, mine_ref, other_ref, shrink_ref, *refs):
    *state, solution_out, residual_out = refs
    half = mine_ref.shape[0]
    for local, at, total_ref in zip((slice(0, half), slice(half, None)), half_slices(half), (mine_ref, other_ref)):
        solution_out[at, :], residual_out[at, :], _ = update(inv_count, local, total_ref, shrink_ref, *state)


def body(genotype, allele_freq, shrink, right_side):
    xs = lax.axis_size("animal") // CORES
    inv_count = 1.0 / (genotype.shape[0] * lax.axis_size("animal"))
    animals, width = genotype.shape
    rhs = right_side.shape[0]
    half = rhs // 2

    def f32(*shape):
        return jax.ShapeDtypeStruct(shape, jnp.float32)

    def call(kernel, name, out_shape, args, scratch=(), mib=6):
        return pl.pallas_call(
            kernel,
            in_specs=[VMEM] * len(args),
            out_specs=jax.tree.map(lambda _: VMEM, out_shape),
            out_shape=out_shape,
            scratch_shapes=list(scratch),
            compiler_params=pltpu.CompilerParams(vmem_limit_bytes=mib * MIB),
            name=name,
        )(*args)

    def terms(n):
        return [pltpu.VMEM((rhs, n), jnp.bfloat16)]

    vec, halves, kept_shape = f32(rhs, width), f32(half, width), f32(rhs, EXTRA)
    ext, own = f32(rhs, 1, animals + EXTRA), f32(half, width + EXTRA)
    line = f32(1, width)

    coded, freq, shrink, residual, scaled, part = pl.pallas_call(
        first_kernel,
        in_specs=[ANY] * 4,
        out_specs=[VMEM] * 6,
        out_shape=[pltpu.VMEM((animals, width), jnp.bfloat16), line, line, vec, vec, ext],
        scratch_shapes=[
            pltpu.VMEM((animals, width), jnp.float32),
            pltpu.VMEM((rhs, width), jnp.float32),
            pltpu.VMEM((width,), jnp.float32),
            pltpu.VMEM((width,), jnp.float32),
            pltpu.VMEM((2 * rhs, width), jnp.bfloat16),
            pltpu.SemaphoreType.DMA((animals // BLOCK,)),
            pltpu.SemaphoreType.DMA((3,)),
        ],
        compiler_params=pltpu.CompilerParams(vmem_limit_bytes=32 * MIB),
        name="first_rows",
    )(*[pltpu.with_memory_space_constraint(v, pltpu.HBM) for v in (genotype, allele_freq, shrink, right_side)])
    coded = pltpu.with_memory_space_constraint(coded, pltpu.VMEM)

    def marker_sum(part):
        got = lax.all_to_all(part, "marker", 0, 0, tiled=True)
        spread = call(spread_kernel, "spread", f32(*got.shape), [got])
        return lax.all_to_all(spread, "marker", 0, 0, tiled=True)

    swap = [(x * CORES + c, x * CORES + 1 - c) for x in range(xs) for c in range(CORES)]

    def to_other(v):
        return lax.ppermute(v, "animal", swap)

    def shift(v, d):
        return lax.ppermute(
            v, "animal", [(x * CORES + c, (x + d) % xs * CORES + c) for x in range(xs) for c in range(CORES)]
        )

    solution = ()
    old = []
    for step in range(ITERS):
        total = marker_sum(part)
        first = step == 0
        shared = [total, freq, coded]
        other = call(
            functools.partial(other_columns, first), "other_columns", own, shared + old[1:], terms(animals)
        )
        other = to_other(other)
        *old, mine = call(
            functools.partial(mine_columns, first), "mine_columns",
            [vec, f32(rhs, animals), kept_shape, own], shared + [scaled] + old, terms(animals),
        )
        direction, _, kept = old
        mine = call(add_kernel, "add", own, [mine, other])
        mine = call(add_kernel, "add", own, [mine] + [shift(mine, d) for d in range(1, xs)])
        other = to_other(mine)
        state = [shrink, direction, residual, kept, *solution]
        if step == ITERS - 1:
            return tuple(call(functools.partial(last_kernel, inv_count), "last", [vec, vec], [mine, other] + state))
        half_part = f32(half, 1, animals + EXTRA)
        outs = call(
            functools.partial(mine_rows, inv_count), "mine_rows", [halves, halves, halves, half_part],
            [freq, coded, mine] + state, terms(width),
        )
        *solution, residual, scaled, part = call(
            functools.partial(other_rows, inv_count), "other_rows", [vec, vec, vec, ext],
            [freq, coded, *outs, other] + state, terms(width),
        )


def solution(mesh):
    placed = (P("animal", "marker"), P("marker"), P("marker"), P(None, "marker"))
    return jax.shard_map(
        body,
        mesh=mesh,
        in_specs=placed,
        out_specs=(P(None, "marker"), P(None, "marker")),
        check_vma=False,
    )
```

```python
import functools

import jax
import jax.numpy as jnp
from jax import lax
from jax.experimental import pallas as pl
from jax.experimental.pallas import tpu as pltpu
from jax.sharding import PartitionSpec as P

ITERS = 4
CORES = 2
DEPTH = 8
EXTRA = 128
BLOCK = 256
PIECE = 512
AHEAD = 2
MIB = 1024 * 1024
VMEM = pl.BlockSpec(memory_space=pltpu.VMEM)
ANY = pl.BlockSpec(memory_space=pl.ANY)


def half_slices(half):
    core = lax.axis_index("animal") % CORES
    return pl.ds(core * half, half), pl.ds((1 - core) * half, half)


def lanes(*columns):
    at = lax.broadcasted_iota(jnp.int32, (columns[0].shape[0], EXTRA), 1)
    out = jnp.zeros(at.shape, jnp.float32)
    for i, column in enumerate(columns):
        out = jnp.where(at == i, column, out)
    return out


def put_terms(v, terms_ref):
    rows = v.shape[0]
    hi = v.astype(jnp.bfloat16)
    terms_ref[:rows] = hi
    terms_ref[rows:] = (v - hi.astype(jnp.float32)).astype(jnp.bfloat16)


def row_sum(v):
    return jnp.sum(v, axis=1, keepdims=True)


def folded(both):
    half = both.shape[0] // 2
    return both[:half] + both[half:]


def product(terms_ref, block):
    return folded(jnp.dot(terms_ref[...], block, preferred_element_type=jnp.float32))


def blocks(extent, block=BLOCK):
    return [pl.ds(i * block, block) for i in range(extent // block)]


def first_kernel(
    geno_ref, freq_ref, shrink_ref, right_ref,
    coded_ref, turned_ref, freq_out, shrink_out, residual_out, scaled_out, part_ref,
    stage, right, freq_line, shrink_line, terms_ref, geno_sems, small_sems,
):
    animals = coded_ref.shape[0]
    half = right_ref.shape[0] // 2
    pairs = ((right_ref, right), (freq_ref, freq_line), (shrink_ref, shrink_line))
    small = [pltpu.make_async_copy(src, dst, small_sems.at[i]) for i, (src, dst) in enumerate(pairs)]
    spots = blocks(animals, PIECE)
    copies = [
        pltpu.make_async_copy(geno_ref.at[at, :], stage.at[at, :], geno_sems.at[i]) for i, at in enumerate(spots)
    ]
    for copy in small + copies[:AHEAD]:
        copy.start()
    for copy in small:
        copy.wait()
    freq = freq_line[...].reshape(1, -1)
    shrink = shrink_line[...].reshape(1, -1)
    freq_out[...] = freq
    shrink_out[...] = shrink
    mine, other = half_slices(half)
    precond = 2.0 * freq * (1.0 - freq) + shrink
    residual_out[:half] = right[mine, :]
    residual_out[half:] = right[other, :]
    scaled_out[...] = residual_out[...] / precond
    residual = right[...]
    scaled = residual / precond
    extra = lanes(row_sum(residual * scaled), row_sum(shrink * scaled * scaled))
    part_ref[:, :, animals:] = extra[:, None, :]
    put_terms(scaled, terms_ref)
    offset = row_sum(2.0 * freq * scaled)
    for i, at in enumerate(spots):
        copies[i].wait()
        if i + AHEAD < len(copies):
            copies[i + AHEAD].start()
        block = stage[at, :].astype(jnp.bfloat16)
        coded_ref[at, :] = block
        turned = block.T
        turned_ref[:, at] = turned
        part_ref[:, :, at] = (product(terms_ref, turned) - offset)[:, None, :]


def collect_kernel(got_ref, out_ref):
    own = out_ref.shape[0]
    total = got_ref[:own]
    for i in range(own, got_ref.shape[0], own):
        total += got_ref[i : i + own]
    out_ref[...] = total


def spread_kernel(*refs):
    *ins, out_ref = refs
    own = ins[0].shape[0]
    total = ins[0][...]
    for ref in ins[1:]:
        total += ref[...]
    for i in range(0, out_ref.shape[0], own):
        out_ref[i : i + own] = total


def add_kernel(*refs):
    *ins, out_ref = refs
    total = ins[0][...]
    for ref in ins[1:]:
        total += ref[...]
    out_ref[...] = total


def half_columns(vec, coded_ref, freq_ref, out_ref, terms_ref):
    width = coded_ref.shape[1]
    put_terms(vec, terms_ref)
    row_total = row_sum(vec)
    for at in blocks(width):
        out_ref[:, at] = product(terms_ref, coded_ref[:, at]) - 2.0 * freq_ref[:, at] * row_total
    out_ref[:, width:] = lanes(row_sum(vec * vec))


def other_columns(first, total_ref, freq_ref, coded_ref, *refs):
    *old, out_ref, terms_ref = refs
    animals = coded_ref.shape[0]
    half = out_ref.shape[0]
    total = total_ref[half_slices(half)[1], 0, :]
    vec = total[:, :animals]
    if not first:
        rows_ref, kept_ref = old
        beta = total[:, animals : animals + 1] / kept_ref[half:, :1]
        vec += beta * rows_ref[half:, :]
    half_columns(vec, coded_ref, freq_ref, out_ref, terms_ref)


def mine_columns(first, last, total_ref, freq_ref, coded_ref, scaled_ref, *refs):
    *refs, terms_ref = refs
    if not last:
        *refs, rows_out = refs
    *old, direction_out, kept_out, out_ref = refs
    animals = coded_ref.shape[0]
    half = out_ref.shape[0]
    for local, at in zip((slice(0, half), slice(half, None)), half_slices(half)):
        total = total_ref[at, 0, :]
        vec = total[:, :animals]
        rho, square, cross = (total[:, animals + i : animals + i + 1] for i in range(3))
        if first:
            direction_out[local] = scaled_ref[local]
            kept_out[local] = lanes(rho, square)
        else:
            direction_ref, rows_ref, kept_ref = old
            beta = rho / kept_ref[local, :1]
            vec += beta * rows_ref[local]
            direction_out[local] = scaled_ref[local] + beta * direction_ref[local]
            kept_out[local] = lanes(rho, square + beta * (2.0 * cross + beta * kept_ref[local, 1:2]))
        if local.start == 0:
            mine = vec
        if not last:
            rows_out[local] = vec
    half_columns(mine, coded_ref, freq_ref, out_ref, terms_ref)


def update(inv_count, local, total_ref, shrink_ref, direction_ref, residual_ref, kept_ref, solution_ref=None):
    width = direction_ref.shape[1]
    direction = direction_ref[local]
    image = total_ref[:, :width] * inv_count + shrink_ref[...] * direction
    curve = total_ref[:, width : width + 1] * inv_count + kept_ref[local, 1:2]
    step = kept_ref[local, :1] / curve
    moved = step * direction
    if solution_ref is not None:
        moved += solution_ref[local]
    return moved, residual_ref[local] - step * image, direction


def half_rows(inv_count, local, state, freq_ref, turned_ref, solution_out, residual_out, scaled_out, write, terms_ref):
    animals = turned_ref.shape[1]
    solution, residual, direction = update(inv_count, local, *state)
    freq, shrink = freq_ref[...], state[1][...]
    scaled = residual / (2.0 * freq * (1.0 - freq) + shrink)
    solution_out[...] = solution
    residual_out[...] = residual
    scaled_out[...] = scaled
    put_terms(scaled, terms_ref)
    weighted = shrink * scaled
    offset = row_sum(2.0 * freq * scaled)
    for at in blocks(animals):
        write(at, product(terms_ref, turned_ref[:, at]) - offset)
    write(
        pl.ds(animals, EXTRA),
        lanes(row_sum(residual * scaled), row_sum(weighted * scaled), row_sum(weighted * direction)),
    )


def mine_rows(inv_count, freq_ref, turned_ref, *refs):
    *state, solution_out, residual_out, scaled_out, part_ref, terms_ref = refs
    half = part_ref.shape[0]

    def write(at, value):
        part_ref[:, :, at] = value[:, None, :]

    half_rows(
        inv_count, slice(0, half), state, freq_ref, turned_ref,
        solution_out, residual_out, scaled_out, write, terms_ref,
    )


def other_rows(inv_count, freq_ref, turned_ref, solution_ref, residual_ref, scaled_ref, half_ref, *refs):
    *state, solution_out, residual_out, scaled_out, part_ref, terms_ref = refs
    half = half_ref.shape[0]
    mine, other = half_slices(half)
    part_ref[mine] = half_ref[...]
    solution_out[:half] = solution_ref[...]
    residual_out[:half] = residual_ref[...]
    scaled_out[:half] = scaled_ref[...]

    def write(at, value):
        part_ref[other, :, at] = value[:, None, :]

    top = slice(half, None)
    half_rows(
        inv_count, top, state, freq_ref, turned_ref,
        solution_out.at[top], residual_out.at[top], scaled_out.at[top], write, terms_ref,
    )


def last_kernel(inv_count, mine_ref, other_ref, shrink_ref, *refs):
    *state, solution_out, residual_out = refs
    half = mine_ref.shape[0]
    for local, at, total_ref in zip((slice(0, half), slice(half, None)), half_slices(half), (mine_ref, other_ref)):
        solution_out[at, :], residual_out[at, :], _ = update(inv_count, local, total_ref, shrink_ref, *state)


def body(genotype, allele_freq, shrink, right_side):
    xs = lax.axis_size("animal") // CORES
    inv_count = 1.0 / (genotype.shape[0] * lax.axis_size("animal"))
    animals, width = genotype.shape
    rhs = right_side.shape[0]
    half = rhs // 2

    def f32(*shape):
        return jax.ShapeDtypeStruct(shape, jnp.float32)

    def call(kernel, name, out_shape, args, scratch=(), mib=6):
        return pl.pallas_call(
            kernel,
            in_specs=[VMEM] * len(args),
            out_specs=jax.tree.map(lambda _: VMEM, out_shape),
            out_shape=out_shape,
            scratch_shapes=list(scratch),
            compiler_params=pltpu.CompilerParams(vmem_limit_bytes=mib * MIB),
            name=name,
        )(*args)

    def terms(n):
        return [pltpu.VMEM((rhs, n), jnp.bfloat16)]

    vec, halves, kept_shape = f32(rhs, width), f32(half, width), f32(rhs, EXTRA)
    ext, own = f32(rhs, 1, animals + EXTRA), f32(half, width + EXTRA)
    line = f32(1, width)

    coded, turned, freq, shrink, residual, scaled, part = pl.pallas_call(
        first_kernel,
        in_specs=[ANY] * 4,
        out_specs=[VMEM] * 7,
        out_shape=[
            pltpu.VMEM((animals, width), jnp.bfloat16), pltpu.VMEM((width, animals), jnp.bfloat16), line, line, vec, vec, ext],
        scratch_shapes=[
            pltpu.VMEM((animals, width), jnp.float32),
            pltpu.VMEM((rhs, width), jnp.float32),
            pltpu.VMEM((width,), jnp.float32),
            pltpu.VMEM((width,), jnp.float32),
            pltpu.VMEM((2 * rhs, width), jnp.bfloat16),
            pltpu.SemaphoreType.DMA((animals // PIECE,)),
            pltpu.SemaphoreType.DMA((3,)),
        ],
        compiler_params=pltpu.CompilerParams(vmem_limit_bytes=32 * MIB),
        name="first_rows",
    )(*[pltpu.with_memory_space_constraint(v, pltpu.HBM) for v in (genotype, allele_freq, shrink, right_side)])
    coded, turned = (pltpu.with_memory_space_constraint(v, pltpu.VMEM) for v in (coded, turned))

    ys = lax.axis_size("marker") // DEPTH
    near = [[y * DEPTH + z + o for y in range(ys) for o in range(2)] for z in range(0, DEPTH, 2)]
    count = 2 * ys

    def exchange(v):
        return lax.all_to_all(v, "marker", 0, 0, tiled=True, axis_index_groups=near)

    def far(v, k):
        return lax.ppermute(v, "marker", [(i, i ^ k) for i in range(ys * DEPTH)])

    def marker_sum(part):
        own = call(collect_kernel, "collect", f32(rhs // count, 1, part.shape[2]), [exchange(part)])
        spread = call(spread_kernel, "spread", ext, [own] + [far(own, k) for k in range(2, DEPTH, 2)])
        return exchange(spread)

    swap = [(x * CORES + c, x * CORES + 1 - c) for x in range(xs) for c in range(CORES)]

    def to_other(v):
        return lax.ppermute(v, "animal", swap)

    def shift(v, d):
        return lax.ppermute(
            v, "animal", [(x * CORES + c, (x + d) % xs * CORES + c) for x in range(xs) for c in range(CORES)]
        )

    solution = ()
    old = []
    for step in range(ITERS):
        total = marker_sum(part)
        first, last = step == 0, step == ITERS - 1
        shared = [total, freq, coded]
        other = call(
            functools.partial(other_columns, first), "other_columns", own, shared + old[1:], terms(animals)
        )
        other = to_other(other)
        direction, kept, mine, *rows = call(
            functools.partial(mine_columns, first, last), "mine_columns",
            [vec, kept_shape, own] + ([] if last else [f32(rhs, animals)]), shared + [scaled] + old, terms(animals),
        )
        old = [direction, *rows, kept]
        mine = call(add_kernel, "add", own, [mine, other])
        mine = call(add_kernel, "add", own, [mine] + [shift(mine, d) for d in range(1, xs)])
        other = to_other(mine)
        state = [shrink, direction, residual, kept, *solution]
        if last:
            return tuple(call(functools.partial(last_kernel, inv_count), "last", [vec, vec], [mine, other] + state))
        half_part = f32(half, 1, animals + EXTRA)
        outs = call(
            functools.partial(mine_rows, inv_count), "mine_rows", [halves, halves, halves, half_part],
            [freq, turned, mine] + state, terms(width),
        )
        *solution, residual, scaled, part = call(
            functools.partial(other_rows, inv_count), "other_rows", [vec, vec, vec, ext],
            [freq, turned, *outs, other] + state, terms(width),
        )


def solution(mesh):
    placed = (P("animal", "marker"), P("marker"), P("marker"), P(None, "marker"))
    return jax.shard_map(
        body,
        mesh=mesh,
        in_specs=placed,
        out_specs=(P(None, "marker"), P(None, "marker")),
        check_vma=False,
    )
```

```python
import functools

import jax
import jax.numpy as jnp
from jax import lax
from jax.experimental import pallas as pl
from jax.experimental.pallas import tpu as pltpu
from jax.sharding import PartitionSpec as P

ITERS = 4
CORES = 2
DEPTH = 8
EXTRA = 128
BLOCK = 256
PIECE = 512
AHEAD = 2
MIB = 1024 * 1024
VMEM = pl.BlockSpec(memory_space=pltpu.VMEM)
ANY = pl.BlockSpec(memory_space=pl.ANY)


def half_slices(half):
    core = lax.axis_index("animal") % CORES
    return pl.ds(core * half, half), pl.ds((1 - core) * half, half)


def lanes(*columns):
    at = lax.broadcasted_iota(jnp.int32, (columns[0].shape[0], EXTRA), 1)
    out = jnp.zeros(at.shape, jnp.float32)
    for i, column in enumerate(columns):
        out = jnp.where(at == i, column, out)
    return out


def put_terms(v, terms_ref):
    rows = v.shape[0]
    hi = v.astype(jnp.bfloat16)
    terms_ref[:rows] = hi
    terms_ref[rows:] = (v - hi.astype(jnp.float32)).astype(jnp.bfloat16)


def row_sum(v):
    return jnp.sum(v, axis=1, keepdims=True)


def folded(both):
    half = both.shape[0] // 2
    return both[:half] + both[half:]


def product(terms_ref, block):
    return folded(jnp.dot(terms_ref[...], block, preferred_element_type=jnp.float32))


def blocks(extent, block=BLOCK):
    return [pl.ds(i * block, block) for i in range(extent // block)]


def first_kernel(
    geno_ref, freq_ref, shrink_ref, right_ref,
    coded_ref, turned_ref, freq_out, shrink_out, residual_out, scaled_out, part_ref,
    stage, right, freq_line, shrink_line, terms_ref, geno_sems, small_sems,
):
    animals = coded_ref.shape[0]
    half = right_ref.shape[0] // 2
    pairs = ((right_ref, right), (freq_ref, freq_line), (shrink_ref, shrink_line))
    small = [pltpu.make_async_copy(src, dst, small_sems.at[i]) for i, (src, dst) in enumerate(pairs)]
    spots = blocks(animals, PIECE)
    copies = [
        pltpu.make_async_copy(geno_ref.at[at, :], stage.at[at, :], geno_sems.at[i]) for i, at in enumerate(spots)
    ]
    for copy in small + copies[:AHEAD]:
        copy.start()
    for copy in small:
        copy.wait()
    freq = freq_line[...].reshape(1, -1)
    shrink = shrink_line[...].reshape(1, -1)
    freq_out[...] = freq
    shrink_out[...] = shrink
    mine, other = half_slices(half)
    precond = 2.0 * freq * (1.0 - freq) + shrink
    residual_out[:half] = right[mine, :]
    residual_out[half:] = right[other, :]
    scaled_out[...] = residual_out[...] / precond
    residual = right[...]
    scaled = residual / precond
    extra = lanes(row_sum(residual * scaled), row_sum(shrink * scaled * scaled))
    part_ref[:, :, animals:] = extra[:, None, :]
    put_terms(scaled, terms_ref)
    offset = row_sum(2.0 * freq * scaled)
    for i, at in enumerate(spots):
        copies[i].wait()
        if i + AHEAD < len(copies):
            copies[i + AHEAD].start()
        block = stage[at, :].astype(jnp.bfloat16)
        coded_ref[at, :] = block
        turned = block.T
        turned_ref[:, at] = turned
        part_ref[:, :, at] = (product(terms_ref, turned) - offset)[:, None, :]


def collect_kernel(got_ref, out_ref):
    own = out_ref.shape[0]
    total = got_ref[:own]
    for i in range(own, got_ref.shape[0], own):
        total += got_ref[i : i + own]
    out_ref[...] = total


def spread_kernel(*refs):
    *ins, out_ref = refs
    own = ins[0].shape[0]
    total = ins[0][...]
    for ref in ins[1:]:
        total += ref[...]
    for i in range(0, out_ref.shape[0], own):
        out_ref[i : i + own] = total


def add_kernel(*refs):
    *ins, out_ref = refs
    total = ins[0][...]
    for ref in ins[1:]:
        total += ref[...]
    out_ref[...] = total


def half_columns(vec, coded_ref, freq_ref, out_ref, terms_ref):
    width = coded_ref.shape[1]
    put_terms(vec, terms_ref)
    row_total = row_sum(vec)
    for at in blocks(width):
        out_ref[:, at] = product(terms_ref, coded_ref[:, at]) - 2.0 * freq_ref[:, at] * row_total
    out_ref[:, width:] = lanes(row_sum(vec * vec))


def other_columns(first, total_ref, freq_ref, coded_ref, *refs):
    *old, out_ref, terms_ref = refs
    animals = coded_ref.shape[0]
    half = out_ref.shape[0]
    total = total_ref[half_slices(half)[1], 0, :]
    vec = total[:, :animals]
    if not first:
        rows_ref, kept_ref = old
        beta = total[:, animals : animals + 1] / kept_ref[half:, :1]
        vec += beta * rows_ref[half:, :]
    half_columns(vec, coded_ref, freq_ref, out_ref, terms_ref)


def mine_columns(first, last, total_ref, freq_ref, coded_ref, scaled_ref, *refs):
    *refs, terms_ref = refs
    if not last:
        *refs, rows_out = refs
    *old, direction_out, kept_out, out_ref = refs
    animals = coded_ref.shape[0]
    half = out_ref.shape[0]
    for local, at in zip((slice(0, half), slice(half, None)), half_slices(half)):
        total = total_ref[at, 0, :]
        vec = total[:, :animals]
        rho, square, cross = (total[:, animals + i : animals + i + 1] for i in range(3))
        if first:
            direction_out[local] = scaled_ref[local]
            kept_out[local] = lanes(rho, square)
        else:
            direction_ref, rows_ref, kept_ref = old
            beta = rho / kept_ref[local, :1]
            vec += beta * rows_ref[local]
            direction_out[local] = scaled_ref[local] + beta * direction_ref[local]
            kept_out[local] = lanes(rho, square + beta * (2.0 * cross + beta * kept_ref[local, 1:2]))
        if local.start == 0:
            mine = vec
        if not last:
            rows_out[local] = vec
    half_columns(mine, coded_ref, freq_ref, out_ref, terms_ref)


def update(inv_count, local, total_ref, shrink_ref, direction_ref, residual_ref, kept_ref, solution_ref=None):
    width = direction_ref.shape[1]
    direction = direction_ref[local]
    image = total_ref[:, :width] * inv_count + shrink_ref[...] * direction
    curve = total_ref[:, width : width + 1] * inv_count + kept_ref[local, 1:2]
    step = kept_ref[local, :1] / curve
    moved = step * direction
    if solution_ref is not None:
        moved += solution_ref[local]
    return moved, residual_ref[local] - step * image, direction


def half_rows(inv_count, local, state, freq_ref, turned_ref, solution_out, residual_out, scaled_out, write, terms_ref):
    animals = turned_ref.shape[1]
    solution, residual, direction = update(inv_count, local, *state)
    freq, shrink = freq_ref[...], state[1][...]
    scaled = residual / (2.0 * freq * (1.0 - freq) + shrink)
    solution_out[...] = solution
    residual_out[...] = residual
    scaled_out[...] = scaled
    put_terms(scaled, terms_ref)
    weighted = shrink * scaled
    offset = row_sum(2.0 * freq * scaled)
    for at in blocks(animals):
        write(at, product(terms_ref, turned_ref[:, at]) - offset)
    write(
        pl.ds(animals, EXTRA),
        lanes(row_sum(residual * scaled), row_sum(weighted * scaled), row_sum(weighted * direction)),
    )


def mine_rows(inv_count, freq_ref, turned_ref, *refs):
    *state, solution_out, residual_out, scaled_out, part_ref, terms_ref = refs
    half = part_ref.shape[0]

    def write(at, value):
        part_ref[:, :, at] = value[:, None, :]

    half_rows(
        inv_count, slice(0, half), state, freq_ref, turned_ref,
        solution_out, residual_out, scaled_out, write, terms_ref,
    )


def other_rows(inv_count, freq_ref, turned_ref, solution_ref, residual_ref, scaled_ref, half_ref, *refs):
    *state, solution_out, residual_out, scaled_out, part_ref, terms_ref = refs
    half = half_ref.shape[0]
    mine, other = half_slices(half)
    part_ref[mine] = half_ref[...]
    solution_out[:half] = solution_ref[...]
    residual_out[:half] = residual_ref[...]
    scaled_out[:half] = scaled_ref[...]

    def write(at, value):
        part_ref[other, :, at] = value[:, None, :]

    top = slice(half, None)
    half_rows(
        inv_count, top, state, freq_ref, turned_ref,
        solution_out.at[top], residual_out.at[top], scaled_out.at[top], write, terms_ref,
    )


def last_kernel(inv_count, mine_ref, other_ref, shrink_ref, *refs):
    *state, solution_out, residual_out = refs
    half = mine_ref.shape[0]
    for local, at, total_ref in zip((slice(0, half), slice(half, None)), half_slices(half), (mine_ref, other_ref)):
        solution_out[at, :], residual_out[at, :], _ = update(inv_count, local, total_ref, shrink_ref, *state)


def body(genotype, allele_freq, shrink, right_side):
    xs = lax.axis_size("animal") // CORES
    inv_count = 1.0 / (genotype.shape[0] * lax.axis_size("animal"))
    animals, width = genotype.shape
    rhs = right_side.shape[0]
    half = rhs // 2

    def f32(*shape):
        return jax.ShapeDtypeStruct(shape, jnp.float32)

    def call(kernel, name, out_shape, args, scratch=(), mib=6):
        return pl.pallas_call(
            kernel,
            in_specs=[VMEM] * len(args),
            out_specs=jax.tree.map(lambda _: VMEM, out_shape),
            out_shape=out_shape,
            scratch_shapes=list(scratch),
            compiler_params=pltpu.CompilerParams(vmem_limit_bytes=mib * MIB),
            name=name,
        )(*args)

    def terms(n):
        return [pltpu.VMEM((rhs, n), jnp.bfloat16)]

    vec, halves, kept_shape = f32(rhs, width), f32(half, width), f32(rhs, EXTRA)
    ext, own = f32(rhs, 1, animals + EXTRA), f32(half, width + EXTRA)
    line = f32(1, width)

    coded, turned, freq, shrink, residual, scaled, part = pl.pallas_call(
        first_kernel,
        in_specs=[ANY] * 4,
        out_specs=[VMEM] * 7,
        out_shape=[
            pltpu.VMEM((animals, width), jnp.bfloat16), pltpu.VMEM((width, animals), jnp.bfloat16), line, line, vec, vec, ext],
        scratch_shapes=[
            pltpu.VMEM((animals, width), jnp.float32),
            pltpu.VMEM((rhs, width), jnp.float32),
            pltpu.VMEM((width,), jnp.float32),
            pltpu.VMEM((width,), jnp.float32),
            pltpu.VMEM((2 * rhs, width), jnp.bfloat16),
            pltpu.SemaphoreType.DMA((animals // PIECE,)),
            pltpu.SemaphoreType.DMA((3,)),
        ],
        compiler_params=pltpu.CompilerParams(vmem_limit_bytes=32 * MIB),
        name="first_rows",
    )(*[pltpu.with_memory_space_constraint(v, pltpu.HBM) for v in (genotype, allele_freq, shrink, right_side)])
    coded, turned = (pltpu.with_memory_space_constraint(v, pltpu.VMEM) for v in (coded, turned))

    ys = lax.axis_size("marker") // DEPTH
    near = [[y * DEPTH + z + o for y in range(ys) for o in range(2)] for z in range(0, DEPTH, 2)]
    count = 2 * ys

    def exchange(v):
        return lax.all_to_all(v, "marker", 0, 0, tiled=True, axis_index_groups=near)

    def far(v, k):
        return lax.ppermute(v, "marker", [(i, i ^ k) for i in range(ys * DEPTH)])

    def marker_sum(part):
        own = call(collect_kernel, "collect", f32(rhs // count, 1, part.shape[2]), [exchange(part)])
        spread = call(spread_kernel, "spread", ext, [own] + [far(own, k) for k in (2, 6, 4)])
        return exchange(spread)

    swap = [(x * CORES + c, x * CORES + 1 - c) for x in range(xs) for c in range(CORES)]

    def to_other(v):
        return lax.ppermute(v, "animal", swap)

    def shift(v, d):
        return lax.ppermute(
            v, "animal", [(x * CORES + c, (x ^ d) * CORES + c) for x in range(xs) for c in range(CORES)]
        )

    solution = ()
    old = []
    for step in range(ITERS):
        total = marker_sum(part)
        first, last = step == 0, step == ITERS - 1
        shared = [total, freq, coded]
        other = call(
            functools.partial(other_columns, first), "other_columns", own, shared + old[1:], terms(animals)
        )
        other = to_other(other)
        direction, kept, mine, *rows = call(
            functools.partial(mine_columns, first, last), "mine_columns",
            [vec, kept_shape, own] + ([] if last else [f32(rhs, animals)]), shared + [scaled] + old, terms(animals),
        )
        old = [direction, *rows, kept]
        mine = call(add_kernel, "add", own, [mine, other])
        mine = call(add_kernel, "add", own, [mine] + [shift(mine, d) for d in (1, 3, 2)])
        other = to_other(mine)
        state = [shrink, direction, residual, kept, *solution]
        if last:
            return tuple(call(functools.partial(last_kernel, inv_count), "last", [vec, vec], [mine, other] + state))
        half_part = f32(half, 1, animals + EXTRA)
        outs = call(
            functools.partial(mine_rows, inv_count), "mine_rows", [halves, halves, halves, half_part],
            [freq, turned, mine] + state, terms(width),
        )
        *solution, residual, scaled, part = call(
            functools.partial(other_rows, inv_count), "other_rows", [vec, vec, vec, ext],
            [freq, turned, *outs, other] + state, terms(width),
        )


def solution(mesh):
    placed = (P("animal", "marker"), P("marker"), P("marker"), P(None, "marker"))
    return jax.shard_map(
        body,
        mesh=mesh,
        in_specs=placed,
        out_specs=(P(None, "marker"), P(None, "marker")),
        check_vma=False,
    )
```

```python
import functools

import jax
import jax.numpy as jnp
from jax import lax
from jax.experimental import pallas as pl
from jax.experimental.pallas import tpu as pltpu
from jax.sharding import PartitionSpec as P

ITERS = 4
CORES = 2
DEPTH = 8
EXTRA = 128
BLOCK = 256
PIECE = 512
AHEAD = 2
MIB = 1024 * 1024
VMEM = pl.BlockSpec(memory_space=pltpu.VMEM)
ANY = pl.BlockSpec(memory_space=pl.ANY)


def half_slices(half):
    core = lax.axis_index("animal") % CORES
    return pl.ds(core * half, half), pl.ds((1 - core) * half, half)


def lanes(*columns):
    at = lax.broadcasted_iota(jnp.int32, (columns[0].shape[0], EXTRA), 1)
    out = jnp.zeros(at.shape, jnp.float32)
    for i, column in enumerate(columns):
        out = jnp.where(at == i, column, out)
    return out


def put_terms(v, terms_ref):
    rows = v.shape[0]
    hi = v.astype(jnp.bfloat16)
    terms_ref[:rows] = hi
    terms_ref[rows:] = (v - hi.astype(jnp.float32)).astype(jnp.bfloat16)


def row_sum(v):
    return jnp.sum(v, axis=1, keepdims=True)


def folded(both):
    half = both.shape[0] // 2
    return both[:half] + both[half:]


def product(terms_ref, block):
    return folded(jnp.dot(terms_ref[...], block, preferred_element_type=jnp.float32))


def blocks(extent, block=BLOCK):
    return [pl.ds(i * block, block) for i in range(extent // block)]


def first_kernel(
    geno_ref, freq_ref, shrink_ref, right_ref,
    coded_ref, turned_ref, freq_out, shrink_out, residual_out, scaled_out, part_ref,
    stage, right, freq_line, shrink_line, terms_ref, geno_sems, small_sems,
):
    animals = coded_ref.shape[0]
    half = right_ref.shape[0] // 2
    pairs = ((right_ref, right), (freq_ref, freq_line), (shrink_ref, shrink_line))
    small = [pltpu.make_async_copy(src, dst, small_sems.at[i]) for i, (src, dst) in enumerate(pairs)]
    spots = blocks(animals, PIECE)
    copies = [
        pltpu.make_async_copy(geno_ref.at[at, :], stage.at[at, :], geno_sems.at[i]) for i, at in enumerate(spots)
    ]
    for copy in small + copies[:AHEAD]:
        copy.start()
    for copy in small:
        copy.wait()
    freq = freq_line[...].reshape(1, -1)
    shrink = shrink_line[...].reshape(1, -1)
    freq_out[...] = freq
    shrink_out[...] = shrink
    mine, other = half_slices(half)
    precond = 2.0 * freq * (1.0 - freq) + shrink
    residual_out[:half] = right[mine, :]
    residual_out[half:] = right[other, :]
    scaled_out[...] = residual_out[...] / precond
    residual = right[...]
    scaled = residual / precond
    extra = lanes(row_sum(residual * scaled), row_sum(shrink * scaled * scaled))
    part_ref[:, :, animals:] = extra[:, None, :]
    put_terms(scaled, terms_ref)
    offset = row_sum(2.0 * freq * scaled)
    for i, at in enumerate(spots):
        copies[i].wait()
        if i + AHEAD < len(copies):
            copies[i + AHEAD].start()
        block = stage[at, :].astype(jnp.bfloat16)
        coded_ref[at, :] = block
        turned = block.T
        turned_ref[:, at] = turned
        part_ref[:, :, at] = (product(terms_ref, turned) - offset)[:, None, :]


def collect_kernel(got_ref, out_ref):
    own = out_ref.shape[0]
    total = got_ref[:own]
    for i in range(own, got_ref.shape[0], own):
        total += got_ref[i : i + own]
    out_ref[...] = total


def spread_kernel(*refs):
    *ins, out_ref = refs
    own = ins[0].shape[0]
    total = ins[0][...]
    for ref in ins[1:]:
        total += ref[...]
    for i in range(0, out_ref.shape[0], own):
        out_ref[i : i + own] = total


def add_kernel(*refs):
    *ins, out_ref = refs
    total = ins[0][...]
    for ref in ins[1:]:
        total += ref[...]
    out_ref[...] = total


def half_columns(vec, coded_ref, freq_ref, out_ref, terms_ref):
    width = coded_ref.shape[1]
    put_terms(vec, terms_ref)
    row_total = row_sum(vec)
    for at in blocks(width):
        out_ref[:, at] = product(terms_ref, coded_ref[:, at]) - 2.0 * freq_ref[:, at] * row_total
    out_ref[:, width:] = lanes(row_sum(vec * vec))


def other_columns(first, total_ref, freq_ref, coded_ref, *refs):
    *old, out_ref, terms_ref = refs
    animals = coded_ref.shape[0]
    half = out_ref.shape[0]
    total = total_ref[half_slices(half)[1], 0, :]
    vec = total[:, :animals]
    if not first:
        rows_ref, kept_ref = old
        beta = total[:, animals : animals + 1] / kept_ref[half:, :1]
        vec += beta * rows_ref[half:, :]
    half_columns(vec, coded_ref, freq_ref, out_ref, terms_ref)


def mine_columns(first, last, total_ref, freq_ref, coded_ref, scaled_ref, *refs):
    *refs, terms_ref = refs
    if not last:
        *refs, rows_out = refs
    *old, direction_out, kept_out, out_ref = refs
    animals = coded_ref.shape[0]
    half = out_ref.shape[0]
    for local, at in zip((slice(0, half), slice(half, None)), half_slices(half)):
        total = total_ref[at, 0, :]
        vec = total[:, :animals]
        rho, square, cross = (total[:, animals + i : animals + i + 1] for i in range(3))
        if first:
            direction_out[local] = scaled_ref[local]
            kept_out[local] = lanes(rho, square)
        else:
            direction_ref, rows_ref, kept_ref = old
            beta = rho / kept_ref[local, :1]
            vec += beta * rows_ref[local]
            direction_out[local] = scaled_ref[local] + beta * direction_ref[local]
            kept_out[local] = lanes(rho, square + beta * (2.0 * cross + beta * kept_ref[local, 1:2]))
        if local.start == 0:
            mine = vec
        if not last:
            rows_out[local] = vec
    half_columns(mine, coded_ref, freq_ref, out_ref, terms_ref)


def update(inv_count, local, total_ref, shrink_ref, direction_ref, residual_ref, kept_ref, solution_ref=None):
    width = direction_ref.shape[1]
    direction = direction_ref[local]
    image = total_ref[:, :width] * inv_count + shrink_ref[...] * direction
    curve = total_ref[:, width : width + 1] * inv_count + kept_ref[local, 1:2]
    step = kept_ref[local, :1] / curve
    moved = step * direction
    if solution_ref is not None:
        moved += solution_ref[local]
    return moved, residual_ref[local] - step * image, direction


def half_rows(inv_count, local, state, freq_ref, turned_ref, solution_out, residual_out, scaled_out, write, terms_ref):
    animals = turned_ref.shape[1]
    solution, residual, direction = update(inv_count, local, *state)
    freq, shrink = freq_ref[...], state[1][...]
    scaled = residual / (2.0 * freq * (1.0 - freq) + shrink)
    solution_out[...] = solution
    residual_out[...] = residual
    scaled_out[...] = scaled
    put_terms(scaled, terms_ref)
    weighted = shrink * scaled
    offset = row_sum(2.0 * freq * scaled)
    for at in blocks(animals):
        write(at, product(terms_ref, turned_ref[:, at]) - offset)
    write(
        pl.ds(animals, EXTRA),
        lanes(row_sum(residual * scaled), row_sum(weighted * scaled), row_sum(weighted * direction)),
    )


def mine_rows(inv_count, freq_ref, turned_ref, *refs):
    *state, solution_out, residual_out, scaled_out, part_ref, terms_ref = refs
    half = part_ref.shape[0]

    def write(at, value):
        part_ref[:, :, at] = value[:, None, :]

    half_rows(
        inv_count, slice(0, half), state, freq_ref, turned_ref,
        solution_out, residual_out, scaled_out, write, terms_ref,
    )


def other_rows(inv_count, freq_ref, turned_ref, solution_ref, residual_ref, scaled_ref, half_ref, *refs):
    *state, solution_out, residual_out, scaled_out, part_ref, terms_ref = refs
    half = half_ref.shape[0]
    mine, other = half_slices(half)
    part_ref[mine] = half_ref[...]
    solution_out[:half] = solution_ref[...]
    residual_out[:half] = residual_ref[...]
    scaled_out[:half] = scaled_ref[...]

    def write(at, value):
        part_ref[other, :, at] = value[:, None, :]

    top = slice(half, None)
    half_rows(
        inv_count, top, state, freq_ref, turned_ref,
        solution_out.at[top], residual_out.at[top], scaled_out.at[top], write, terms_ref,
    )


def last_kernel(inv_count, mine_ref, other_ref, shrink_ref, *refs):
    *state, solution_out, residual_out = refs
    half = mine_ref.shape[0]
    for local, at, total_ref in zip((slice(0, half), slice(half, None)), half_slices(half), (mine_ref, other_ref)):
        solution_out[at, :], residual_out[at, :], _ = update(inv_count, local, total_ref, shrink_ref, *state)


def body(genotype, allele_freq, shrink, right_side):
    xs = lax.axis_size("animal") // CORES
    inv_count = 1.0 / (genotype.shape[0] * lax.axis_size("animal"))
    animals, width = genotype.shape
    rhs = right_side.shape[0]
    half = rhs // 2

    def f32(*shape):
        return jax.ShapeDtypeStruct(shape, jnp.float32)

    def call(kernel, name, out_shape, args, scratch=(), mib=6):
        return pl.pallas_call(
            kernel,
            in_specs=[VMEM] * len(args),
            out_specs=jax.tree.map(lambda _: VMEM, out_shape),
            out_shape=out_shape,
            scratch_shapes=list(scratch),
            compiler_params=pltpu.CompilerParams(vmem_limit_bytes=mib * MIB),
            name=name,
        )(*args)

    def terms(n):
        return [pltpu.VMEM((rhs, n), jnp.bfloat16)]

    vec, halves, kept_shape = f32(rhs, width), f32(half, width), f32(rhs, EXTRA)
    ext, own = f32(rhs, 1, animals + EXTRA), f32(half, width + EXTRA)
    line = f32(1, width)

    coded, turned, freq, shrink, residual, scaled, part = pl.pallas_call(
        first_kernel,
        in_specs=[ANY] * 4,
        out_specs=[VMEM] * 7,
        out_shape=[
            pltpu.VMEM((animals, width), jnp.bfloat16), pltpu.VMEM((width, animals), jnp.bfloat16), line, line, vec, vec, ext],
        scratch_shapes=[
            pltpu.VMEM((animals, width), jnp.float32),
            pltpu.VMEM((rhs, width), jnp.float32),
            pltpu.VMEM((width,), jnp.float32),
            pltpu.VMEM((width,), jnp.float32),
            pltpu.VMEM((2 * rhs, width), jnp.bfloat16),
            pltpu.SemaphoreType.DMA((animals // PIECE,)),
            pltpu.SemaphoreType.DMA((3,)),
        ],
        compiler_params=pltpu.CompilerParams(vmem_limit_bytes=32 * MIB),
        name="first_rows",
    )(*[pltpu.with_memory_space_constraint(v, pltpu.HBM) for v in (genotype, allele_freq, shrink, right_side)])
    coded, turned = (pltpu.with_memory_space_constraint(v, pltpu.VMEM) for v in (coded, turned))

    ys = lax.axis_size("marker") // DEPTH
    near = [[y * DEPTH + z + o for o in range(2) for y in (0, 2, 1, 3)] for z in range(0, DEPTH, 2)]
    count = 2 * ys

    def exchange(v):
        return lax.all_to_all(v, "marker", 0, 0, tiled=True, axis_index_groups=near)

    def far(v, k):
        return lax.ppermute(v, "marker", [(i, i ^ k) for i in range(ys * DEPTH)])

    def marker_sum(part):
        own = call(collect_kernel, "collect", f32(rhs // count, 1, part.shape[2]), [exchange(part)])
        spread = call(spread_kernel, "spread", ext, [own] + [far(own, k) for k in (2, 6, 4)])
        return exchange(spread)

    swap = [(x * CORES + c, x * CORES + 1 - c) for x in range(xs) for c in range(CORES)]

    def to_other(v):
        return lax.ppermute(v, "animal", swap)

    def shift(v, d):
        return lax.ppermute(
            v, "animal", [(x * CORES + c, (x ^ d) * CORES + c) for x in range(xs) for c in range(CORES)]
        )

    solution = ()
    old = []
    for step in range(ITERS):
        total = marker_sum(part)
        first, last = step == 0, step == ITERS - 1
        shared = [total, freq, coded]
        other = call(
            functools.partial(other_columns, first), "other_columns", own, shared + old[1:], terms(animals)
        )
        other = to_other(other)
        direction, kept, mine, *rows = call(
            functools.partial(mine_columns, first, last), "mine_columns",
            [vec, kept_shape, own] + ([] if last else [f32(rhs, animals)]), shared + [scaled] + old, terms(animals),
        )
        old = [direction, *rows, kept]
        mine = call(add_kernel, "add", own, [mine, other])
        mine = call(add_kernel, "add", own, [mine] + [shift(mine, d) for d in (1, 3, 2)])
        other = to_other(mine)
        state = [shrink, direction, residual, kept, *solution]
        if last:
            return tuple(call(functools.partial(last_kernel, inv_count), "last", [vec, vec], [mine, other] + state))
        half_part = f32(half, 1, animals + EXTRA)
        outs = call(
            functools.partial(mine_rows, inv_count), "mine_rows", [halves, halves, halves, half_part],
            [freq, turned, mine] + state, terms(width),
        )
        *solution, residual, scaled, part = call(
            functools.partial(other_rows, inv_count), "other_rows", [vec, vec, vec, ext],
            [freq, turned, *outs, other] + state, terms(width),
        )


def solution(mesh):
    placed = (P("animal", "marker"), P("marker"), P("marker"), P(None, "marker"))
    return jax.shard_map(
        body,
        mesh=mesh,
        in_specs=placed,
        out_specs=(P(None, "marker"), P(None, "marker")),
        check_vma=False,
    )
```

```python
import functools

import jax
import jax.numpy as jnp
from jax import lax
from jax.experimental import pallas as pl
from jax.experimental.pallas import tpu as pltpu
from jax.sharding import PartitionSpec as P

ITERS = 4
CORES = 2
DEPTH = 8
EXTRA = 128
BLOCK = 256
PIECE = 512
AHEAD = 2
MIB = 1024 * 1024
VMEM = pl.BlockSpec(memory_space=pltpu.VMEM)
ANY = pl.BlockSpec(memory_space=pl.ANY)


def half_slices(half):
    core = lax.axis_index("animal") % CORES
    return pl.ds(core * half, half), pl.ds((1 - core) * half, half)


def lanes(*columns):
    at = lax.broadcasted_iota(jnp.int32, (columns[0].shape[0], EXTRA), 1)
    out = jnp.zeros(at.shape, jnp.float32)
    for i, column in enumerate(columns):
        out = jnp.where(at == i, column, out)
    return out


def put_terms(v, terms_ref):
    rows = v.shape[0]
    hi = v.astype(jnp.bfloat16)
    terms_ref[:rows] = hi
    terms_ref[rows:] = (v - hi.astype(jnp.float32)).astype(jnp.bfloat16)


def row_sum(v):
    return jnp.sum(v, axis=1, keepdims=True)


def folded(both):
    half = both.shape[0] // 2
    return both[:half] + both[half:]


def product(terms_ref, block):
    return folded(jnp.dot(terms_ref[...], block, preferred_element_type=jnp.float32))


def blocks(extent, block=BLOCK):
    return [pl.ds(i * block, block) for i in range(extent // block)]


def first_kernel(
    geno_ref, freq_ref, shrink_ref, right_ref,
    coded_ref, turned_ref, freq_out, shrink_out, residual_out, scaled_out, part_ref,
    stage, right, freq_line, shrink_line, terms_ref, geno_sems, small_sems,
):
    animals = coded_ref.shape[0]
    half = right_ref.shape[0] // 2
    pairs = ((right_ref, right), (freq_ref, freq_line), (shrink_ref, shrink_line))
    small = [pltpu.make_async_copy(src, dst, small_sems.at[i]) for i, (src, dst) in enumerate(pairs)]
    spots = blocks(animals, PIECE)
    copies = [
        pltpu.make_async_copy(geno_ref.at[at, :], stage.at[at, :], geno_sems.at[i]) for i, at in enumerate(spots)
    ]
    for copy in small + copies[:AHEAD]:
        copy.start()
    for copy in small:
        copy.wait()
    freq = freq_line[...].reshape(1, -1)
    shrink = shrink_line[...].reshape(1, -1)
    freq_out[...] = freq
    shrink_out[...] = shrink
    mine, other = half_slices(half)
    precond = 2.0 * freq * (1.0 - freq) + shrink
    residual_out[:half] = right[mine, :]
    residual_out[half:] = right[other, :]
    scaled_out[...] = residual_out[...] / precond
    residual = right[...]
    scaled = residual / precond
    extra = lanes(row_sum(residual * scaled), row_sum(shrink * scaled * scaled))
    part_ref[:, :, animals:] = extra[:, None, :]
    put_terms(scaled, terms_ref)
    offset = row_sum(2.0 * freq * scaled)
    for i, at in enumerate(spots):
        copies[i].wait()
        if i + AHEAD < len(copies):
            copies[i + AHEAD].start()
        block = stage[at, :].astype(jnp.bfloat16)
        coded_ref[at, :] = block
        turned = block.T
        turned_ref[:, at] = turned
        part_ref[:, :, at] = (product(terms_ref, turned) - offset)[:, None, :]


def collect_kernel(got_ref, out_ref):
    own = out_ref.shape[0]
    total = got_ref[:own]
    for i in range(own, got_ref.shape[0], own):
        total += got_ref[i : i + own]
    out_ref[...] = total


def spread_kernel(*refs):
    *ins, out_ref = refs
    own = ins[0].shape[0]
    total = ins[0][...]
    for ref in ins[1:]:
        total += ref[...]
    for i in range(0, out_ref.shape[0], own):
        out_ref[i : i + own] = total


def add_kernel(*refs):
    *ins, out_ref = refs
    total = ins[0][...]
    for ref in ins[1:]:
        total += ref[...]
    out_ref[...] = total


def half_columns(vec, coded_ref, freq_ref, out_ref, terms_ref):
    width = coded_ref.shape[1]
    put_terms(vec, terms_ref)
    row_total = row_sum(vec)
    for at in blocks(width):
        out_ref[:, at] = product(terms_ref, coded_ref[:, at]) - 2.0 * freq_ref[:, at] * row_total
    out_ref[:, width:] = lanes(row_sum(vec * vec))


def other_columns(first, total_ref, freq_ref, coded_ref, *refs):
    *old, out_ref, terms_ref = refs
    animals = coded_ref.shape[0]
    half = out_ref.shape[0]
    total = total_ref[half_slices(half)[1], 0, :]
    vec = total[:, :animals]
    if not first:
        rows_ref, kept_ref = old
        beta = total[:, animals : animals + 1] / kept_ref[half:, :1]
        vec += beta * rows_ref[half:, :]
    half_columns(vec, coded_ref, freq_ref, out_ref, terms_ref)


def mine_columns(first, last, total_ref, freq_ref, coded_ref, scaled_ref, *refs):
    *refs, terms_ref = refs
    if not last:
        *refs, rows_out = refs
    *old, direction_out, kept_out, out_ref = refs
    animals = coded_ref.shape[0]
    half = out_ref.shape[0]
    for local, at in zip((slice(0, half), slice(half, None)), half_slices(half)):
        total = total_ref[at, 0, :]
        vec = total[:, :animals]
        rho, square, cross = (total[:, animals + i : animals + i + 1] for i in range(3))
        if first:
            direction_out[local] = scaled_ref[local]
            kept_out[local] = lanes(rho, square)
        else:
            direction_ref, rows_ref, kept_ref = old
            beta = rho / kept_ref[local, :1]
            vec += beta * rows_ref[local]
            direction_out[local] = scaled_ref[local] + beta * direction_ref[local]
            kept_out[local] = lanes(rho, square + beta * (2.0 * cross + beta * kept_ref[local, 1:2]))
        if local.start == 0:
            mine = vec
        if not last:
            rows_out[local] = vec
    half_columns(mine, coded_ref, freq_ref, out_ref, terms_ref)


def update(inv_count, local, total_ref, shrink_ref, direction_ref, residual_ref, kept_ref, solution_ref=None):
    width = direction_ref.shape[1]
    direction = direction_ref[local]
    image = total_ref[:, :width] * inv_count + shrink_ref[...] * direction
    curve = total_ref[:, width : width + 1] * inv_count + kept_ref[local, 1:2]
    step = kept_ref[local, :1] / curve
    moved = step * direction
    if solution_ref is not None:
        moved += solution_ref[local]
    return moved, residual_ref[local] - step * image, direction


def half_rows(inv_count, local, state, freq_ref, turned_ref, solution_out, residual_out, scaled_out, write, terms_ref):
    animals = turned_ref.shape[1]
    solution, residual, direction = update(inv_count, local, *state)
    freq, shrink = freq_ref[...], state[1][...]
    scaled = residual / (2.0 * freq * (1.0 - freq) + shrink)
    solution_out[...] = solution
    residual_out[...] = residual
    scaled_out[...] = scaled
    put_terms(scaled, terms_ref)
    weighted = shrink * scaled
    offset = row_sum(2.0 * freq * scaled)
    for at in blocks(animals):
        write(at, product(terms_ref, turned_ref[:, at]) - offset)
    write(
        pl.ds(animals, EXTRA),
        lanes(row_sum(residual * scaled), row_sum(weighted * scaled), row_sum(weighted * direction)),
    )


def mine_rows(inv_count, freq_ref, turned_ref, *refs):
    *state, solution_out, residual_out, scaled_out, part_ref, terms_ref = refs
    half = part_ref.shape[0]

    def write(at, value):
        part_ref[:, :, at] = value[:, None, :]

    half_rows(
        inv_count, slice(0, half), state, freq_ref, turned_ref,
        solution_out, residual_out, scaled_out, write, terms_ref,
    )


def other_rows(inv_count, freq_ref, turned_ref, solution_ref, residual_ref, scaled_ref, half_ref, *refs):
    *state, solution_out, residual_out, scaled_out, part_ref, terms_ref = refs
    half = half_ref.shape[0]
    mine, other = half_slices(half)
    part_ref[mine] = half_ref[...]
    solution_out[:half] = solution_ref[...]
    residual_out[:half] = residual_ref[...]
    scaled_out[:half] = scaled_ref[...]

    def write(at, value):
        part_ref[other, :, at] = value[:, None, :]

    top = slice(half, None)
    half_rows(
        inv_count, top, state, freq_ref, turned_ref,
        solution_out.at[top], residual_out.at[top], scaled_out.at[top], write, terms_ref,
    )


def last_mine(inv_count, mine_ref, *refs):
    *state, solution_out, residual_out = refs
    solution_out[...], residual_out[...], _ = update(inv_count, slice(0, mine_ref.shape[0]), mine_ref, *state)


def last_other(inv_count, mine_solution, mine_residual, other_ref, *refs):
    *state, solution_out, residual_out = refs
    half = other_ref.shape[0]
    mine, other = half_slices(half)
    solution_out[mine, :] = mine_solution[...]
    residual_out[mine, :] = mine_residual[...]
    solution_out[other, :], residual_out[other, :], _ = update(inv_count, slice(half, None), other_ref, *state)


def body(genotype, allele_freq, shrink, right_side):
    xs = lax.axis_size("animal") // CORES
    inv_count = 1.0 / (genotype.shape[0] * lax.axis_size("animal"))
    animals, width = genotype.shape
    rhs = right_side.shape[0]
    half = rhs // 2

    def f32(*shape):
        return jax.ShapeDtypeStruct(shape, jnp.float32)

    def call(kernel, name, out_shape, args, scratch=(), mib=6):
        return pl.pallas_call(
            kernel,
            in_specs=[VMEM] * len(args),
            out_specs=jax.tree.map(lambda _: VMEM, out_shape),
            out_shape=out_shape,
            scratch_shapes=list(scratch),
            compiler_params=pltpu.CompilerParams(vmem_limit_bytes=mib * MIB),
            name=name,
        )(*args)

    def terms(n):
        return [pltpu.VMEM((rhs, n), jnp.bfloat16)]

    vec, halves, kept_shape = f32(rhs, width), f32(half, width), f32(rhs, EXTRA)
    ext, own = f32(rhs, 1, animals + EXTRA), f32(half, width + EXTRA)
    line = f32(1, width)

    coded, turned, freq, shrink, residual, scaled, part = pl.pallas_call(
        first_kernel,
        in_specs=[ANY] * 4,
        out_specs=[VMEM] * 7,
        out_shape=[
            pltpu.VMEM((animals, width), jnp.bfloat16), pltpu.VMEM((width, animals), jnp.bfloat16), line, line, vec, vec, ext],
        scratch_shapes=[
            pltpu.VMEM((animals, width), jnp.float32),
            pltpu.VMEM((rhs, width), jnp.float32),
            pltpu.VMEM((width,), jnp.float32),
            pltpu.VMEM((width,), jnp.float32),
            pltpu.VMEM((2 * rhs, width), jnp.bfloat16),
            pltpu.SemaphoreType.DMA((animals // PIECE,)),
            pltpu.SemaphoreType.DMA((3,)),
        ],
        compiler_params=pltpu.CompilerParams(vmem_limit_bytes=32 * MIB),
        name="first_rows",
    )(*[pltpu.with_memory_space_constraint(v, pltpu.HBM) for v in (genotype, allele_freq, shrink, right_side)])
    coded, turned = (pltpu.with_memory_space_constraint(v, pltpu.VMEM) for v in (coded, turned))

    ys = lax.axis_size("marker") // DEPTH
    near = [[y * DEPTH + z + o for o in range(2) for y in (0, 2, 1, 3)] for z in range(0, DEPTH, 2)]
    count = 2 * ys

    def exchange(v):
        return lax.all_to_all(v, "marker", 0, 0, tiled=True, axis_index_groups=near)

    def far(v, k):
        return lax.ppermute(v, "marker", [(i, i ^ k) for i in range(ys * DEPTH)])

    def marker_sum(part):
        own = call(collect_kernel, "collect", f32(rhs // count, 1, part.shape[2]), [exchange(part)])
        spread = call(spread_kernel, "spread", ext, [own] + [far(own, k) for k in (2, 6, 4)])
        return exchange(spread)

    swap = [(x * CORES + c, x * CORES + 1 - c) for x in range(xs) for c in range(CORES)]

    def to_other(v):
        return lax.ppermute(v, "animal", swap)

    def shift(v, d):
        return lax.ppermute(
            v, "animal", [(x * CORES + c, (x ^ d) * CORES + c) for x in range(xs) for c in range(CORES)]
        )

    solution = ()
    old = []
    for step in range(ITERS):
        total = marker_sum(part)
        first, last = step == 0, step == ITERS - 1
        shared = [total, freq, coded]
        other = call(
            functools.partial(other_columns, first), "other_columns", own, shared + old[1:], terms(animals)
        )
        other = to_other(other)
        direction, kept, mine, *rows = call(
            functools.partial(mine_columns, first, last), "mine_columns",
            [vec, kept_shape, own] + ([] if last else [f32(rhs, animals)]), shared + [scaled] + old, terms(animals),
        )
        old = [direction, *rows, kept]
        mine = call(add_kernel, "add", own, [mine, other])
        mine = call(add_kernel, "add", own, [mine] + [shift(mine, d) for d in (1, 3, 2)])
        other = to_other(mine)
        state = [shrink, direction, residual, kept, *solution]
        if last:
            outs = call(functools.partial(last_mine, inv_count), "last_mine", [halves, halves], [mine] + state)
            return tuple(
                call(functools.partial(last_other, inv_count), "last_other", [vec, vec], [*outs, other] + state)
            )
        half_part = f32(half, 1, animals + EXTRA)
        outs = call(
            functools.partial(mine_rows, inv_count), "mine_rows", [halves, halves, halves, half_part],
            [freq, turned, mine] + state, terms(width),
        )
        *solution, residual, scaled, part = call(
            functools.partial(other_rows, inv_count), "other_rows", [vec, vec, vec, ext],
            [freq, turned, *outs, other] + state, terms(width),
        )


def solution(mesh):
    placed = (P("animal", "marker"), P("marker"), P("marker"), P(None, "marker"))
    return jax.shard_map(
        body,
        mesh=mesh,
        in_specs=placed,
        out_specs=(P(None, "marker"), P(None, "marker")),
        check_vma=False,
    )
```
